128 devices in a mesh: row: 8 (over y_hi, z), col: 16 (over y_lo, x, core).
Axes of the slice: x: 4, y: 4 (y_hi: 2, y_lo: 2; y = y_hi * 2 + y_lo), z: 4, core: 2. Of those that a mesh axis runs over, the one named last changes fastest.
Arguments:
- tensor: bfloat16 [8, 4096, 2048], P('row', 'col'), may hold values from -6 to 6
- density: bfloat16 [2048, 16384], P('row', 'col'), may hold values from -0.125 to 0.125
- tensor_mask: int32 [32, 16], replicated, may hold values 0 or 1
- density_mask: int32 [16, 128], replicated, may hold values 0 or 1
- block_sizes: int32 [128], replicated, may hold values from 64 to 128
Outputs:
- contracted: bfloat16 [8, 4096, 16384], P('row', None, 'col')
The draws below stay inside these ranges and needn't reach their ends.
All inputs are finite; a program needn't handle non-finite values.
Results may differ from the reference program's by a relative error of at most 0.001.
Values may be sent and summed in bfloat16 or wider, within the bound.
No kernel may reach another device: no remote copies, remote signals or barrier semaphores. Data moves between devices by JAX's collectives and lax.ppermute only.
A program may use at most 256 MiB of HBM per device.

```python
import jax
import jax.numpy as jnp
from jax import lax

BLK = 128
MU_BLOCKS = 32
NU_BLOCKS = 16
NAUX = 8
MU = 4096
NU = 2048
SIG_BLOCKS = 128
SIG = 16384


def plant(entries, rng, least, top_value):
    dims = entries.shape
    index_at = [jax.random.randint(jax.random.fold_in(rng, axis), (), 0, dims[axis]) for axis in range(len(dims))]
    entries = entries.at[tuple(index_at)].set(least)
    longest = dims.index(max(dims))
    index_at[longest] = (index_at[longest] + 1) % dims[longest]
    return entries.at[tuple(index_at)].set(top_value)


def steps_of(own_key, dims, split, smallest, high):
    def one(position, parts):
        heights = jax.random.uniform(jax.random.fold_in(jax.random.fold_in(own_key, 6), position), (parts,), jnp.float32, smallest / len(split), high / len(split))
        return jnp.repeat(jnp.exp(heights), dims[position] // parts).reshape((-1,) + (1,) * (len(dims) - position - 1))

    level = one(*split[0])
    for cut in split[1:]:
        level = level * one(*cut)
    return level


def bell_draw(stream_key, extent, width, limit, pieces=(), kind=jnp.bfloat16):
    values = jax.random.normal(stream_key, extent, jnp.float32) * width
    if len(pieces) > 0:
        values = steps_of(stream_key, extent, pieces, -0.22, 0.18) * values
    return jnp.clip(values, min=-limit, max=limit).astype(kind)


def setup_inputs(seed: int = 0) -> dict:
    arg_keys = jax.random.split(jax.random.key(seed), 6)
    tensor = bell_draw(arg_keys[0], (NAUX, MU, NU), 1.0, 6.0, ((0, 8), (1, 16)))
    density = bell_draw(arg_keys[1], (NU, SIG), NU ** -0.5, 0.125, ((0, 8), (1, 16)))
    tensor_mask = plant((jax.random.randint(arg_keys[2], (MU_BLOCKS, NU_BLOCKS), 0, 3) < 2).astype(jnp.int32), jax.random.fold_in(arg_keys[2], 1), 0, 1)
    density_mask = plant((jax.random.randint(arg_keys[3], (NU_BLOCKS, SIG_BLOCKS), 0, 3) < 2).astype(jnp.int32), jax.random.fold_in(arg_keys[3], 1), 0, 1)
    block_sizes = plant(jax.random.randint(arg_keys[4], (SIG_BLOCKS,), BLK // 2, BLK + 1), jax.random.fold_in(arg_keys[4], 1), BLK // 2, BLK).astype(jnp.int32)
    return dict(tensor=tensor, density=density, tensor_mask=tensor_mask, density_mask=density_mask, block_sizes=block_sizes)


def expand_keep(block_mask, row_live, col_live):
    wide = jnp.repeat(jnp.repeat(block_mask == 1, BLK, 0), BLK, 1)
    return wide & row_live[:, None] & col_live[None, :]


def reference(tensor, density, tensor_mask, density_mask, block_sizes):
    within = jnp.arange(BLK, dtype=jnp.int32)
    slot_live = (within[None, :] < block_sizes[:, None]).reshape(-1)
    tensor_keep = expand_keep(tensor_mask, slot_live[:MU], slot_live[:NU])
    density_keep = expand_keep(density_mask, slot_live[:NU], slot_live)
    kept_density = jnp.where(density_keep, density, jnp.zeros((), density.dtype))

    def contract(aux_slab):
        kept_slab = jnp.where(tensor_keep, aux_slab, jnp.zeros((), aux_slab.dtype))
        return jnp.dot(kept_slab, kept_density, preferred_element_type=jnp.float32).astype(jnp.bfloat16)

    return lax.map(contract, tensor)
```

```python
import functools

import jax
import jax.numpy as jnp
from jax import lax
from jax.experimental import pallas as pl
from jax.experimental.pallas import tpu as pltpu
from jax.sharding import Mesh, PartitionSpec as P

BLK = 128
ROW = ("yh", "z")
COL = ("yl", "x", "c")
MIB = 1024 * 1024
VMEM = pl.BlockSpec(memory_space=pltpu.VMEM)
SMEM = pl.BlockSpec(memory_space=pltpu.SMEM)
ANY = pl.BlockSpec(memory_space=pl.ANY)
HBM = pl.BlockSpec(memory_space=pltpu.HBM)
ROUND = pl.CostEstimate(flops=3 * 10**10, bytes_accessed=0, transcendentals=0)


def after(value, *earlier):
    return lax.optimization_barrier((value, *earlier))[0]


def passed(value, axis):
    n = lax.axis_size(axis)
    pairs = [(i * 2 + c, ((i + 1 - 2 * c) % n) * 2 + c) for i in range(n) for c in range(2)]
    return lax.ppermute(value, (axis, "c"), pairs)


def swapped(value, axis):
    return lax.ppermute(value, axis, [(0, 1), (1, 0)])


def offset_of(sizes_ref, count):
    return lax.fori_loop(0, count, lambda i, s: s + sizes_ref[i], jnp.int32(0))


def at_row():
    return lax.axis_index("yh") * lax.axis_size("z") + lax.axis_index("z")


def at_col():
    nx, nc = lax.axis_size("x"), lax.axis_size("c")
    return (lax.axis_index("yl") * nx + lax.axis_index("x")) * nc + lax.axis_index("c")


def wrapped(value, n):
    return lax.rem(value + n, n)


def chunk_place(dy, d, dc):
    nx = lax.axis_size("x")
    c = wrapped(lax.axis_index("c") + dc, 2)
    x = wrapped(lax.axis_index("x") - (1 - 2 * c) * d, nx)
    return (wrapped(lax.axis_index("yl") + dy, 2) * nx + x) * 2 + c


def panel_place(dy, d):
    nz = lax.axis_size("z")
    z = wrapped(lax.axis_index("z") - (1 - 2 * lax.axis_index("c")) * d, nz)
    return wrapped(lax.axis_index("yh") + dy, 2) * nz + z


def start_body(sizes_hbm, t_mask_hbm, d_mask_hbm, tensor_hbm, density_hbm, own_ref, rho_ref,
               sizes_ref, t_mask_ref, d_mask_ref, tensor_ref, density_ref, sem):
    copies = [
        pltpu.make_async_copy(src, dst, sem.at[i])
        for i, (src, dst) in enumerate([
            (sizes_hbm, sizes_ref), (t_mask_hbm, t_mask_ref), (d_mask_hbm, d_mask_ref),
            (density_hbm, density_ref), (tensor_hbm.at[0], tensor_ref),
        ])
    ]
    for copy in copies:
        copy.start()
    row_at, col_at = at_row(), at_col()
    wide = own_ref.shape[1]
    slot = lax.broadcasted_iota(jnp.int32, (BLK, 2 * BLK), 0)
    target = lax.broadcasted_iota(jnp.int32, (BLK, 2 * BLK), 1)
    row = lax.broadcasted_iota(jnp.int32, (BLK, BLK), 0)
    col = lax.broadcasted_iota(jnp.int32, (BLK, BLK), 1)
    own_ref[...] = jnp.zeros_like(own_ref)
    for copy in copies[:4]:
        copy.wait()
    rows, cols = rho_ref.shape
    for i in range(rows // BLK):
        nu = row_at * (rows // BLK) + i
        for j in range(cols // BLK):
            sig = col_at * (cols // BLK) + j
            live = jnp.where(d_mask_ref[nu, sig] == 1, sizes_ref[nu], 0)
            at = (pl.ds(i * BLK, BLK), pl.ds(j * BLK, BLK))
            part = density_ref[at].astype(jnp.float32)
            keep = (row < live) & (col < sizes_ref[sig])
            rho_ref[at] = jnp.where(keep, part, 0.0).astype(rho_ref.dtype)
    copies[4].wait()
    blocks = own_ref.shape[0] // BLK
    offset = jnp.int32(0)
    for n in range(tensor_ref.shape[1] // BLK):
        size = sizes_ref[n]
        start = jnp.minimum(offset // BLK * BLK, wide - 2 * BLK)
        start = pl.multiple_of(start, BLK)
        pick = (target == slot + (offset - start)) & (slot < size)
        pick = pick.astype(jnp.float32).astype(jnp.bfloat16)
        for m in range(blocks):
            mu = col_at * blocks + m
            live = jnp.where(t_mask_ref[n, mu] == 1, sizes_ref[mu], 0)
            at = pl.ds(m * BLK, BLK)
            part = tensor_ref[at, n * BLK : (n + 1) * BLK].astype(jnp.float32)
            part = jnp.where(row < live, part, 0.0).astype(jnp.bfloat16)
            moved = jnp.dot(part, pick, preferred_element_type=jnp.float32)
            own_ref[at, pl.ds(start, 2 * BLK)] += moved.astype(jnp.bfloat16)
        offset = offset + size


def start(sizes, t_mask, d_mask, tensor, density, wide):
    _, rows, nu = tensor.shape
    return pl.pallas_call(
        start_body,
        in_specs=[HBM] * 5,
        out_specs=[VMEM] * 2,
        out_shape=[
            jax.ShapeDtypeStruct((rows, wide), tensor.dtype),
            jax.ShapeDtypeStruct(density.shape, density.dtype),
        ],
        scratch_shapes=[
            pltpu.SMEM(sizes.shape, jnp.int32),
            pltpu.SMEM(t_mask.shape[::-1], jnp.int32),
            pltpu.SMEM(d_mask.shape, jnp.int32),
            pltpu.VMEM((rows, nu), tensor.dtype),
            pltpu.VMEM(density.shape, density.dtype),
            pltpu.SemaphoreType.DMA((5,)),
        ],
        compiler_params=pltpu.CompilerParams(vmem_limit_bytes=60 * MIB),
        cost_estimate=ROUND,
    )(sizes, t_mask.T, d_mask, tensor, density)


def gather_body(origins, first, sizes_hbm, *refs):
    panels = len(origins)
    out_ref, sizes_ref, sem = refs[panels + (0 if first else 1) :]
    copy = pltpu.make_async_copy(sizes_hbm, sizes_ref, sem)
    copy.start()
    rows = refs[0].shape[0]
    wide = out_ref.shape[0]
    window = rows + 16
    target = lax.broadcasted_iota(jnp.int32, (window, rows), 0)
    slot = lax.broadcasted_iota(jnp.int32, (window, rows), 1)
    if first:
        out_ref[...] = jnp.zeros_like(out_ref)
    per = rows // BLK
    copy.wait()
    for k, origin in enumerate(origins):
        at = panel_place(*origin) * per
        offset = offset_of(sizes_ref, at)
        start = pl.multiple_of(jnp.minimum(offset // 16 * 16, wide - window), 16)
        base = offset - start
        pick = jnp.zeros((window, rows), jnp.bool_)
        for b in range(per):
            size = sizes_ref[at + b]
            inside = (slot >= b * BLK) & (slot < b * BLK + size)
            pick = pick | (inside & (target == slot - b * BLK + base))
            base = base + size
        pick = pick.astype(jnp.float32).astype(jnp.bfloat16)
        moved = jnp.dot(pick, refs[k][...], preferred_element_type=jnp.float32)
        out_ref[pl.ds(start, window), :] += moved.astype(out_ref.dtype)


def gather(sizes, panels, wide, out):
    cols = panels[0][1].shape[1]
    first = out is None
    return pl.pallas_call(
        functools.partial(gather_body, [o for o, _ in panels], first),
        in_specs=[HBM] + [VMEM] * (len(panels) + (0 if first else 1)),
        out_specs=VMEM,
        out_shape=jax.ShapeDtypeStruct((wide, cols), jnp.bfloat16),
        scratch_shapes=[pltpu.SMEM(sizes.shape, jnp.int32), pltpu.SemaphoreType.DMA],
        input_output_aliases={} if first else {1 + len(panels): 0},
        compiler_params=pltpu.CompilerParams(vmem_limit_bytes=8 * MIB),
        cost_estimate=ROUND,
    )(sizes, *[p for _, p in panels], *([] if first else [out]))


def product_body(origins, split, first, rho_ref, *refs):
    count = len(origins)
    a_refs = refs[: sum(split)]
    out_ref, o_buf, o_sem = refs[sum(split) + (0 if first else 1) :]
    tall = o_buf.shape[1]

    def out_copy(i):
        start = pl.multiple_of(chunk_place(*origins[i]) * tall, tall)
        return pltpu.make_async_copy(
            o_buf.at[i % 2], out_ref.at[pl.ds(start, tall)], o_sem.at[i % 2]
        )

    k = 0
    for i, parts in enumerate(split):
        if i >= 2:
            out_copy(i - 2).wait()
        rows = [a_refs[k + part][...] for part in range(parts)]
        k += parts
        rows = rows[0] if parts == 1 else jnp.concatenate(rows, axis=0)
        o_buf[i % 2] = jnp.dot(
            rows, rho_ref[...], preferred_element_type=jnp.float32
        ).astype(o_buf.dtype)
        out_copy(i).start()
    for i in range(max(count - 2, 0), count):
        out_copy(i).wait()


def product(rho, chunks, out, shape):
    split = [len(parts) for _, parts in chunks]
    flat = [p for _, parts in chunks for p in parts]
    tall, wide = sum(p.shape[0] for p in chunks[0][1]), rho.shape[0]
    count, first = len(chunks), out is None
    return pl.pallas_call(
        functools.partial(product_body, [o for o, _ in chunks], split, first),
        in_specs=[VMEM] * (1 + len(flat)) + ([] if first else [ANY]),
        out_specs=ANY,
        scratch_shapes=[
            pltpu.VMEM((2, tall, shape[1]), jnp.bfloat16),
            pltpu.SemaphoreType.DMA((2,)),
        ],
        out_shape=jax.ShapeDtypeStruct(shape, jnp.bfloat16),
        input_output_aliases={} if first else {1 + len(flat): 0},
        compiler_params=pltpu.CompilerParams(vmem_limit_bytes=8 * MIB),
        cost_estimate=pl.CostEstimate(
            flops=2 * count * tall * wide * shape[1],
            bytes_accessed=2 * count * tall * shape[1],
            transcendentals=0,
        ),
    )(rho, *flat, *([] if first else [out]))


def contract(wide, out, tensor, density, tensor_mask, density_mask, block_sizes):
    nz, nx = lax.axis_size("z"), lax.axis_size("x")
    own, rho = start(block_sizes, tensor_mask, density_mask, tensor, density, wide)
    r1, c_own = passed(own, "x"), swapped(own, "c")
    t0, s1 = swapped(rho, "yh"), passed(rho, "z")

    def add(panels, out, *earlier):
        return gather(after(block_sizes, *earlier), panels, wide, out)

    rho_all = add([((0, 0), rho)], None, own)
    s2 = passed(after(s1, rho_all), "z")
    t1, y0 = passed(after(t0, rho_all), "z"), swapped(after(own, t0, rho_all), "yl")
    r2, c_r1 = passed(after(r1, rho_all), "x"), swapped(after(r1, c_own), "c")
    rho_all = add([((0, 1), s1), ((1, 0), t0)], rho_all, r1)
    s3, t2, r3 = passed(after(s2, rho_all), "z"), passed(after(t1, rho_all), "z"), passed(after(r2, rho_all), "x")
    c_r2 = swapped(after(r2, c_r1), "c")
    rho_all = add([((0, 2), s2), ((1, 1), t1)], rho_all, r2, c_r1)
    t3 = passed(after(t2, rho_all), "z")
    q1, q2 = passed(after(y0, r3, rho_all), "x"), swapped(after(r2, y0, rho_all), "yl")
    c_y0, c_r3 = swapped(after(y0, c_r2), "c"), swapped(after(r3, s3), "c")
    rho_all = add([((0, 3), s3), ((1, 2), t2)], rho_all, r3, y0, c_r2)
    rho_all = add([((1, 3), t3)], rho_all)
    shape = (own.shape[0] * 2 * nx * 2, density.shape[1])
    out = product(rho_all, [
        ((0, 0, 0), (own,)), ((0, 1, 0), (r1,)), ((0, 2, 0), (r2,)), ((1, 0, 0), (y0,)),
        ((0, 3, 0), (r3,)), ((0, 0, 1), (c_own,)), ((0, 1, 1), (c_r1,)), ((0, 2, 1), (c_r2,)),
    ], out, shape)
    q1 = after(q1, out)
    q3 = passed(after(q2, q1), "x")
    c_q1 = swapped(after(q1, c_r3), "c")
    c_q2 = swapped(after(q2, c_y0), "c")
    out = product(rho_all, [
        ((1, 0, 1), (c_y0,)), ((0, 3, 1), (c_r3,)), ((1, 1, 0), (q1,)), ((1, 1, 1), (c_q1,)),
        ((1, 2, 0), (q2,)), ((1, 2, 1), (c_q2,)),
    ], out, shape)
    q3 = after(q3, out)
    c_q3 = swapped(q3, "c")
    out = product(rho_all, [((1, 3, 0), (q3,))], out, shape)
    out = product(rho_all, [((1, 3, 1), (c_q3,))], out, shape)
    return out, q1


def local(*args):
    nu, sizes = args[0].shape[2], args[4]
    narrow = nu * 13 // 16
    out, late = contract(narrow, None, *args)
    more = jnp.sum(after(sizes, late)[: nu // BLK]) > narrow

    def again(carry):
        return jnp.bool_(False), contract(nu, carry[1], *args)[0]

    return lax.while_loop(lambda carry: carry[0], again, (more, out))[1][None]


def solution(mesh):
    rows, cols = mesh.devices.shape
    nz, nx, nc = rows // 2, cols // 4, 2
    fine = Mesh(mesh.devices.reshape(2, nz, 2, nx, nc), ("yh", "z", "yl", "x", "c"))
    placed = (P(ROW, COL, None), P(ROW, COL), P(), P(), P())
    return jax.shard_map(
        local, mesh=fine, in_specs=placed, out_specs=P(ROW, None, COL), check_vma=False
    )
```

```python
import functools

import jax
import jax.numpy as jnp
from jax import lax
from jax.experimental import pallas as pl
from jax.experimental.pallas import tpu as pltpu
from jax.sharding import Mesh, PartitionSpec as P

BLK = 128
ROW = ("yh", "z")
COL = ("yl", "x", "c")
MIB = 1024 * 1024
VMEM = pl.BlockSpec(memory_space=pltpu.VMEM)
SMEM = pl.BlockSpec(memory_space=pltpu.SMEM)
ANY = pl.BlockSpec(memory_space=pl.ANY)
HBM = pl.BlockSpec(memory_space=pltpu.HBM)
ROUND = pl.CostEstimate(flops=5 * 10**9, bytes_accessed=0, transcendentals=0)


def after(value, *earlier):
    return lax.optimization_barrier((value, *earlier))[0]


def passed(value, axis):
    n = lax.axis_size(axis)
    pairs = [(i * 2 + c, ((i + 1 - 2 * c) % n) * 2 + c) for i in range(n) for c in range(2)]
    return lax.ppermute(value, (axis, "c"), pairs)


def swapped(value, axis):
    return lax.ppermute(value, axis, [(0, 1), (1, 0)])


def offset_of(sizes_ref, count):
    return lax.fori_loop(0, count, lambda i, s: s + sizes_ref[i], jnp.int32(0))


def at_row():
    return lax.axis_index("yh") * lax.axis_size("z") + lax.axis_index("z")


def at_col():
    nx, nc = lax.axis_size("x"), lax.axis_size("c")
    return (lax.axis_index("yl") * nx + lax.axis_index("x")) * nc + lax.axis_index("c")


def wrapped(value, n):
    return lax.rem(value + n, n)


def chunk_place(dy, dx, dc):
    nx, c = lax.axis_size("x"), lax.axis_index("c")
    x = wrapped(lax.axis_index("x") - (1 - 2 * c) * dx, nx)
    return (wrapped(lax.axis_index("yl") + dy, 2) * nx + x) * 2 + wrapped(c + dc, 2)


def panel_place(dy, d):
    nz = lax.axis_size("z")
    z = wrapped(lax.axis_index("z") - (1 - 2 * lax.axis_index("c")) * d, nz)
    return wrapped(lax.axis_index("yh") + dy, 2) * nz + z


def start_body(sizes_hbm, t_mask_hbm, d_mask_hbm, tensor_hbm, density_hbm, own_ref, rho_ref,
               live_ref, sizes_ref, t_mask_ref, d_mask_ref, tensor_ref, density_ref, sem):
    copies = [
        pltpu.make_async_copy(src, dst, sem.at[i])
        for i, (src, dst) in enumerate([
            (sizes_hbm, sizes_ref), (t_mask_hbm, t_mask_ref), (d_mask_hbm, d_mask_ref),
            (density_hbm, density_ref), (tensor_hbm.at[0], tensor_ref),
        ])
    ]
    for copy in copies:
        copy.start()
    row_at, col_at = at_row(), at_col()
    wide = own_ref.shape[1]
    slot = lax.broadcasted_iota(jnp.int32, (BLK, 2 * BLK), 0)
    target = lax.broadcasted_iota(jnp.int32, (BLK, 2 * BLK), 1)
    row = lax.broadcasted_iota(jnp.int32, (BLK, BLK), 0)
    col = lax.broadcasted_iota(jnp.int32, (BLK, BLK), 1)
    own_ref[...] = jnp.zeros_like(own_ref)
    for copy in copies[:4]:
        copy.wait()
    rows, cols = rho_ref.shape
    for i in range(rows // BLK):
        nu = row_at * (rows // BLK) + i
        for j in range(cols // BLK):
            sig = col_at * (cols // BLK) + j
            live = jnp.where(d_mask_ref[nu, sig] == 1, sizes_ref[nu], 0)
            at = (pl.ds(i * BLK, BLK), pl.ds(j * BLK, BLK))
            part = density_ref[at].astype(jnp.float32)
            keep = (row < live) & (col < sizes_ref[sig])
            rho_ref[at] = jnp.where(keep, part, 0.0).astype(rho_ref.dtype)
    copies[4].wait()
    blocks = own_ref.shape[0] // BLK
    offset = jnp.int32(0)
    for n in range(tensor_ref.shape[1] // BLK):
        size = sizes_ref[n]
        start = jnp.minimum(offset // BLK * BLK, wide - 2 * BLK)
        start = pl.multiple_of(start, BLK)
        pick = (target == slot + (offset - start)) & (slot < size)
        pick = pick.astype(jnp.float32).astype(jnp.bfloat16)
        for m in range(blocks):
            mu = col_at * blocks + m
            live = jnp.where(t_mask_ref[n, mu] == 1, sizes_ref[mu], 0)
            at = pl.ds(m * BLK, BLK)
            part = tensor_ref[at, n * BLK : (n + 1) * BLK].astype(jnp.float32)
            part = jnp.where(row < live, part, 0.0).astype(jnp.bfloat16)
            moved = jnp.dot(part, pick, preferred_element_type=jnp.float32)
            own_ref[at, pl.ds(start, 2 * BLK)] += moved.astype(jnp.bfloat16)
        offset = offset + size
    live_ref[...] = jnp.full_like(live_ref, offset)


def start(sizes, t_mask, d_mask, tensor, density, wide):
    _, rows, nu = tensor.shape
    return pl.pallas_call(
        start_body,
        in_specs=[HBM] * 5,
        out_specs=[VMEM] * 3,
        out_shape=[
            jax.ShapeDtypeStruct((rows, wide), tensor.dtype),
            jax.ShapeDtypeStruct(density.shape, density.dtype),
            jax.ShapeDtypeStruct((8, BLK), jnp.int32),
        ],
        scratch_shapes=[
            pltpu.SMEM(sizes.shape, jnp.int32),
            pltpu.SMEM(t_mask.shape[::-1], jnp.int32),
            pltpu.SMEM(d_mask.shape, jnp.int32),
            pltpu.VMEM((rows, nu), tensor.dtype),
            pltpu.VMEM(density.shape, density.dtype),
            pltpu.SemaphoreType.DMA((5,)),
        ],
        compiler_params=pltpu.CompilerParams(vmem_limit_bytes=48 * MIB),
        cost_estimate=ROUND,
    )(sizes, t_mask.T, d_mask, tensor, density)


def gather_body(origins, first, sizes_hbm, *refs):
    panels = len(origins)
    out_ref, sizes_ref, sem = refs[panels + (0 if first else 1) :]
    copy = pltpu.make_async_copy(sizes_hbm, sizes_ref, sem)
    copy.start()
    rows = refs[0].shape[0]
    wide = out_ref.shape[0]
    window = rows + 16
    target = lax.broadcasted_iota(jnp.int32, (window, rows), 0)
    slot = lax.broadcasted_iota(jnp.int32, (window, rows), 1)
    if first:
        out_ref[...] = jnp.zeros_like(out_ref)
    per = rows // BLK
    copy.wait()
    for k, origin in enumerate(origins):
        at = panel_place(*origin) * per
        offset = offset_of(sizes_ref, at)
        start = pl.multiple_of(jnp.minimum(offset // 16 * 16, wide - window), 16)
        base = offset - start
        pick = jnp.zeros((window, rows), jnp.bool_)
        for b in range(per):
            size = sizes_ref[at + b]
            inside = (slot >= b * BLK) & (slot < b * BLK + size)
            pick = pick | (inside & (target == slot - b * BLK + base))
            base = base + size
        pick = pick.astype(jnp.float32).astype(jnp.bfloat16)
        moved = jnp.dot(pick, refs[k][...], preferred_element_type=jnp.float32)
        out_ref[pl.ds(start, window), :] += moved.astype(out_ref.dtype)


def gather(sizes, panels, wide, out):
    cols = panels[0][1].shape[1]
    first = out is None
    return pl.pallas_call(
        functools.partial(gather_body, [o for o, _ in panels], first),
        in_specs=[HBM] + [VMEM] * (len(panels) + (0 if first else 1)),
        out_specs=VMEM,
        out_shape=jax.ShapeDtypeStruct((wide, cols), jnp.bfloat16),
        scratch_shapes=[pltpu.SMEM(sizes.shape, jnp.int32), pltpu.SemaphoreType.DMA],
        input_output_aliases={} if first else {1 + len(panels): 0},
        compiler_params=pltpu.CompilerParams(vmem_limit_bytes=8 * MIB),
        cost_estimate=ROUND,
    )(sizes, *[p for _, p in panels], *([] if first else [out]))


def product_body(origins, split, first, live_ref, rho_ref, *refs):
    count = len(origins)
    a_refs = refs[: sum(split)]
    out_ref, token_ref, o_buf, o_sem = refs[sum(split) + (0 if first else 1) :]
    tall = o_buf.shape[1]

    def out_copy(i):
        start = pl.multiple_of(chunk_place(*origins[i]) * tall, tall)
        return pltpu.make_async_copy(
            o_buf.at[i % 2], out_ref.at[pl.ds(start, tall)], o_sem.at[i % 2]
        )

    k = 0
    for i, parts in enumerate(split):
        if i >= 2:
            out_copy(i - 2).wait()
        rows = [a_refs[k + part][...] for part in range(parts)]
        k += parts
        rows = rows[0] if parts == 1 else jnp.concatenate(rows, axis=0)
        o_buf[i % 2] = jnp.dot(
            rows, rho_ref[...], preferred_element_type=jnp.float32
        ).astype(o_buf.dtype)
        out_copy(i).start()
    for i in range(max(count - 2, 0), count):
        out_copy(i).wait()
    token_ref[...] = live_ref[...]


def product(live, rho, chunks, out, shape):
    split = [len(parts) for _, parts in chunks]
    flat = [p for _, parts in chunks for p in parts]
    tall, wide = sum(p.shape[0] for p in chunks[0][1]), rho.shape[0]
    count, first = len(chunks), out is None
    return pl.pallas_call(
        functools.partial(product_body, [o for o, _ in chunks], split, first),
        in_specs=[VMEM] * (2 + len(flat)) + ([] if first else [ANY]),
        out_specs=[ANY, VMEM],
        scratch_shapes=[
            pltpu.VMEM((2, tall, shape[1]), jnp.bfloat16),
            pltpu.SemaphoreType.DMA((2,)),
        ],
        out_shape=[
            jax.ShapeDtypeStruct(shape, jnp.bfloat16),
            jax.ShapeDtypeStruct(live.shape, live.dtype),
        ],
        input_output_aliases={} if first else {2 + len(flat): 0},
        compiler_params=pltpu.CompilerParams(vmem_limit_bytes=8 * MIB),
        cost_estimate=pl.CostEstimate(
            flops=2 * count * tall * wide * shape[1],
            bytes_accessed=2 * count * tall * shape[1],
            transcendentals=0,
        ),
    )(live, rho, *flat, *([] if first else [out]))


def contract(wide, out, tensor, density, tensor_mask, density_mask, block_sizes):
    nz, nx = lax.axis_size("z"), lax.axis_size("x")
    own, rho, live = start(block_sizes, tensor_mask, density_mask, tensor, density, wide)

    def add(panels, out, *earlier):
        return gather(after(block_sizes, *earlier), panels, wide, out)

    a1, c_own = passed(own, "x"), swapped(own, "c")
    s1, t0 = passed(rho, "z"), swapped(rho, "yh")
    y0 = swapped(own, "yl")
    g = add([((0, 0), rho)], None, own)
    b1, a2 = passed(after(c_own, g), "x"), passed(after(a1, g), "x")
    s2, t1 = passed(after(s1, g), "z"), passed(after(t0, g), "z")
    g = add([((0, 1), s1), ((1, 0), t0)], g, c_own, a1)
    s3, t2 = passed(after(s2, g), "z"), passed(after(t1, g), "z")
    c_a1 = swapped(after(a1, b1, g), "c")
    g = add([((0, 2), s2), ((1, 1), t1)], g, b1)
    qa, q2 = passed(after(y0, g), "x"), swapped(after(a2, y0, g), "yl")
    c_y0 = swapped(after(y0, s3, g), "c")
    c_b1 = swapped(after(b1, c_a1, g), "c")
    t3 = passed(after(t2, g), "z")
    g = add([((0, 3), s3), ((1, 2), t2)], g, y0, a2, c_a1)
    qb = passed(after(c_y0, g), "x")
    c_a2 = swapped(after(a2, c_b1, g), "c")
    c_qa = swapped(after(qa, c_y0, g), "c")
    g = add([((1, 3), t3)], g, c_b1, c_y0, qa)
    shape = (own.shape[0] * 4 * nx, density.shape[1])
    out, live = product(live, g, [
        ((0, 0, 0), (own,)), ((0, 0, 1), (c_own,)), ((0, 1, 0), (a1,)), ((0, 1, 1), (b1,)),
        ((1, 0, 0), (y0,)), ((1, 0, 1), (c_y0,)), ((0, 2, 0), (a2,)), ((0, -1, 1), (c_a1,)),
    ], out, shape)
    c_q2 = swapped(after(q2, live), "c")
    c_qb = swapped(after(qb, live), "c")
    out, live = product(live, g, [
        ((0, -1, 0), (c_b1,)), ((0, 2, 1), (c_a2,)), ((1, 1, 0), (qa,)), ((1, -1, 1), (c_qa,)),
    ], out, shape)
    out, live = product(live, g, [
        ((1, 2, 0), (q2,)), ((1, 2, 1), (c_q2,)), ((1, 1, 1), (qb,)), ((1, -1, 0), (c_qb,)),
    ], out, shape)
    return out, live


def local(*args):
    nu = args[0].shape[2]
    narrow = nu * 7 // 8
    out, live = contract(narrow, None, *args)
    more = live[0, 0] > narrow

    def again(carry):
        return jnp.bool_(False), contract(nu, carry[1], *args)[0]

    return lax.while_loop(lambda carry: carry[0], again, (more, out))[1][None]


def solution(mesh):
    rows, cols = mesh.devices.shape
    nz, nx, nc = rows // 2, cols // 4, 2
    fine = Mesh(mesh.devices.reshape(2, nz, 2, nx, nc), ("yh", "z", "yl", "x", "c"))
    placed = (P(ROW, COL, None), P(ROW, COL), P(), P(), P())
    return jax.shard_map(
        local, mesh=fine, in_specs=placed, out_specs=P(ROW, None, COL), check_vma=False
    )
```

```python
import functools

import jax
import jax.numpy as jnp
from jax import lax
from jax.experimental import pallas as pl
from jax.experimental.pallas import tpu as pltpu
from jax.sharding import Mesh, PartitionSpec as P

BLK = 128
ROW = ("yh", "z")
COL = ("yl", "x", "c")
MIB = 1024 * 1024
VMEM = pl.BlockSpec(memory_space=pltpu.VMEM)
SMEM = pl.BlockSpec(memory_space=pltpu.SMEM)
ANY = pl.BlockSpec(memory_space=pl.ANY)
HBM = pl.BlockSpec(memory_space=pltpu.HBM)
ROUND = pl.CostEstimate(flops=5 * 10**9, bytes_accessed=0, transcendentals=0)


def after(value, *earlier):
    return lax.optimization_barrier((value, *earlier))[0]


def passed(value, axis):
    n = lax.axis_size(axis)
    pairs = [(i * 2 + c, ((i + 1 - 2 * c) % n) * 2 + c) for i in range(n) for c in range(2)]
    return lax.ppermute(value, (axis, "c"), pairs)


def swapped(value, axis):
    return lax.ppermute(value, axis, [(0, 1), (1, 0)])


def offset_of(sizes_ref, count):
    return lax.fori_loop(0, count, lambda i, s: s + sizes_ref[i], jnp.int32(0))


def at_row():
    return lax.axis_index("yh") * lax.axis_size("z") + lax.axis_index("z")


def at_col():
    nx, nc = lax.axis_size("x"), lax.axis_size("c")
    return (lax.axis_index("yl") * nx + lax.axis_index("x")) * nc + lax.axis_index("c")


def wrapped(value, n):
    return lax.rem(value + n, n)


def chunk_place(dy, dx, dc):
    nx, c = lax.axis_size("x"), lax.axis_index("c")
    x = wrapped(lax.axis_index("x") - (1 - 2 * c) * dx, nx)
    return (wrapped(lax.axis_index("yl") + dy, 2) * nx + x) * 2 + wrapped(c + dc, 2)


def panel_place(dy, d):
    nz = lax.axis_size("z")
    z = wrapped(lax.axis_index("z") - (1 - 2 * lax.axis_index("c")) * d, nz)
    return wrapped(lax.axis_index("yh") + dy, 2) * nz + z


def start_body(sizes_hbm, t_mask_hbm, d_mask_hbm, tensor_hbm, density_hbm, own_ref, rho_ref,
               live_ref, sizes_ref, t_mask_ref, d_mask_ref, tensor_ref, density_ref, sem):
    copies = [
        pltpu.make_async_copy(src, dst, sem.at[i])
        for i, (src, dst) in enumerate([
            (sizes_hbm, sizes_ref), (t_mask_hbm, t_mask_ref), (d_mask_hbm, d_mask_ref),
            (density_hbm, density_ref), (tensor_hbm.at[0], tensor_ref),
        ])
    ]
    for copy in copies:
        copy.start()
    row_at, col_at = at_row(), at_col()
    wide = own_ref.shape[1]
    slot = lax.broadcasted_iota(jnp.int32, (BLK, 2 * BLK), 0)
    target = lax.broadcasted_iota(jnp.int32, (BLK, 2 * BLK), 1)
    row = lax.broadcasted_iota(jnp.int32, (BLK, BLK), 0)
    col = lax.broadcasted_iota(jnp.int32, (BLK, BLK), 1)
    own_ref[...] = jnp.zeros_like(own_ref)
    for copy in copies[:4]:
        copy.wait()
    rows, cols = rho_ref.shape
    for i in range(rows // BLK):
        nu = row_at * (rows // BLK) + i
        for j in range(cols // BLK):
            sig = col_at * (cols // BLK) + j
            live = jnp.where(d_mask_ref[nu, sig] == 1, sizes_ref[nu], 0)
            at = (pl.ds(i * BLK, BLK), pl.ds(j * BLK, BLK))
            part = density_ref[at].astype(jnp.float32)
            keep = (row < live) & (col < sizes_ref[sig])
            rho_ref[at] = jnp.where(keep, part, 0.0).astype(rho_ref.dtype)
    copies[4].wait()
    blocks = own_ref.shape[0] // BLK
    offset = jnp.int32(0)
    for n in range(tensor_ref.shape[1] // BLK):
        size = sizes_ref[n]
        start = jnp.minimum(offset // BLK * BLK, wide - 2 * BLK)
        start = pl.multiple_of(start, BLK)
        pick = (target == slot + (offset - start)) & (slot < size)
        pick = pick.astype(jnp.float32).astype(jnp.bfloat16)
        for m in range(blocks):
            mu = col_at * blocks + m
            live = jnp.where(t_mask_ref[n, mu] == 1, sizes_ref[mu], 0)
            at = pl.ds(m * BLK, BLK)
            part = tensor_ref[at, n * BLK : (n + 1) * BLK].astype(jnp.float32)
            part = jnp.where(row < live, part, 0.0).astype(jnp.bfloat16)
            moved = jnp.dot(part, pick, preferred_element_type=jnp.float32)
            own_ref[at, pl.ds(start, 2 * BLK)] += moved.astype(jnp.bfloat16)
        offset = offset + size
    live_ref[...] = jnp.full_like(live_ref, offset)


def start(sizes, t_mask, d_mask, tensor, density, wide):
    _, rows, nu = tensor.shape
    return pl.pallas_call(
        start_body,
        in_specs=[HBM] * 5,
        out_specs=[VMEM] * 3,
        out_shape=[
            jax.ShapeDtypeStruct((rows, wide), tensor.dtype),
            jax.ShapeDtypeStruct(density.shape, density.dtype),
            jax.ShapeDtypeStruct((8, BLK), jnp.int32),
        ],
        scratch_shapes=[
            pltpu.SMEM(sizes.shape, jnp.int32),
            pltpu.SMEM(t_mask.shape[::-1], jnp.int32),
            pltpu.SMEM(d_mask.shape, jnp.int32),
            pltpu.VMEM((rows, nu), tensor.dtype),
            pltpu.VMEM(density.shape, density.dtype),
            pltpu.SemaphoreType.DMA((5,)),
        ],
        compiler_params=pltpu.CompilerParams(vmem_limit_bytes=48 * MIB),
        cost_estimate=ROUND,
    )(sizes, t_mask.T, d_mask, tensor, density)


def in_spans(columns, total, span):
    if span == total:
        columns(0, 0)
    else:
        lax.fori_loop(0, total // span, columns, 0)


def gather_body(origins, first, span, sizes_hbm, *refs):
    panels = len(origins)
    out_ref, sizes_ref, sem = refs[panels + (0 if first else 1) :]
    copy = pltpu.make_async_copy(sizes_hbm, sizes_ref, sem)
    copy.start()
    rows = refs[0].shape[0]
    wide = out_ref.shape[0]
    window = rows + 16
    target = lax.broadcasted_iota(jnp.int32, (window, rows), 0)
    slot = lax.broadcasted_iota(jnp.int32, (window, rows), 1)
    if first:
        out_ref[...] = jnp.zeros_like(out_ref)
    per = rows // BLK
    copy.wait()
    for k, origin in enumerate(origins):
        at = panel_place(*origin) * per
        offset = offset_of(sizes_ref, at)
        start = pl.multiple_of(jnp.minimum(offset // 16 * 16, wide - window), 16)
        base = offset - start
        pick = jnp.zeros((window, rows), jnp.bool_)
        for b in range(per):
            size = sizes_ref[at + b]
            inside = (slot >= b * BLK) & (slot < b * BLK + size)
            pick = pick | (inside & (target == slot - b * BLK + base))
            base = base + size
        pick = pick.astype(jnp.float32).astype(jnp.bfloat16)

        def columns(n, carry):
            at = slice(None) if span == out_ref.shape[1] else pl.ds(pl.multiple_of(n * span, span), span)
            moved = jnp.dot(pick, refs[k][:, at], preferred_element_type=jnp.float32)
            out_ref[pl.ds(start, window), at] += moved.astype(out_ref.dtype)
            return carry

        in_spans(columns, out_ref.shape[1], span)


def gather(sizes, panels, wide, out, span):
    cols = panels[0][1].shape[1]
    first = out is None
    return pl.pallas_call(
        functools.partial(gather_body, [o for o, _ in panels], first, span),
        in_specs=[HBM] + [VMEM] * (len(panels) + (0 if first else 1)),
        out_specs=VMEM,
        out_shape=jax.ShapeDtypeStruct((wide, cols), jnp.bfloat16),
        scratch_shapes=[pltpu.SMEM(sizes.shape, jnp.int32), pltpu.SemaphoreType.DMA],
        input_output_aliases={} if first else {1 + len(panels): 0},
        compiler_params=pltpu.CompilerParams(vmem_limit_bytes=8 * MIB),
        cost_estimate=ROUND,
    )(sizes, *[p for _, p in panels], *([] if first else [out]))


def product_body(origins, first, span, live_ref, rho_ref, *refs):
    count = len(origins)
    a_refs = refs[:count]
    out_ref, token_ref, o_buf, o_sem = refs[count + (0 if first else 1) :]
    tall = o_buf.shape[1]

    def out_copy(i):
        start = pl.multiple_of(chunk_place(*origins[i]) * tall, tall)
        return pltpu.make_async_copy(
            o_buf.at[i % 2], out_ref.at[pl.ds(start, tall)], o_sem.at[i % 2]
        )

    for i in range(count):
        if i >= 2:
            out_copy(i - 2).wait()

        def columns(n, carry):
            at = slice(None) if span == out_ref.shape[1] else pl.ds(pl.multiple_of(n * span, span), span)
            o_buf[i % 2, :, at] = jnp.dot(
                a_refs[i][...], rho_ref[:, at], preferred_element_type=jnp.float32
            ).astype(o_buf.dtype)
            return carry

        in_spans(columns, o_buf.shape[2], span)
        out_copy(i).start()
    for i in range(max(count - 2, 0), count):
        out_copy(i).wait()
    token_ref[...] = live_ref[...]


def product(live, rho, chunks, out, shape, span, cost=1):
    flat = [part for _, (part,) in chunks]
    tall, wide = flat[0].shape
    count, first = len(chunks), out is None
    return pl.pallas_call(
        functools.partial(product_body, [o for o, _ in chunks], first, span),
        in_specs=[VMEM] * (2 + len(flat)) + ([] if first else [ANY]),
        out_specs=[ANY, VMEM],
        scratch_shapes=[
            pltpu.VMEM((2, tall, shape[1]), jnp.bfloat16),
            pltpu.SemaphoreType.DMA((2,)),
        ],
        out_shape=[
            jax.ShapeDtypeStruct(shape, jnp.bfloat16),
            jax.ShapeDtypeStruct(live.shape, live.dtype),
        ],
        input_output_aliases={} if first else {2 + len(flat): 0},
        compiler_params=pltpu.CompilerParams(vmem_limit_bytes=42 * MIB),
        cost_estimate=pl.CostEstimate(
            flops=2 * cost * count * tall * wide * shape[1],
            bytes_accessed=2 * cost * count * tall * shape[1],
            transcendentals=0,
        ),
    )(live, rho, *flat, *([] if first else [out]))


def contract(wide, span, out, tensor, density, tensor_mask, density_mask, block_sizes):
    nz, nx = lax.axis_size("z"), lax.axis_size("x")
    own, rho, live = start(block_sizes, tensor_mask, density_mask, tensor, density, wide)

    def add(panels, out, *earlier):
        return gather(after(block_sizes, *earlier), panels, wide, out, span)

    a1, c_own = passed(own, "x"), swapped(own, "c")
    s1, t0 = passed(rho, "z"), swapped(rho, "yh")
    y0 = swapped(own, "yl")
    g = add([((0, 0), rho)], None, own)
    b1 = passed(after(c_own, g), "x")
    s2 = passed(after(s1, g), "z")
    g = add([((0, 1), s1)], g, c_own)
    a2, t1 = passed(after(a1, g), "x"), passed(after(t0, g), "z")
    g = add([((1, 0), t0)], g, a1)
    s3, t2 = passed(after(s2, g), "z"), passed(after(t1, g), "z")
    c_a1 = swapped(after(a1, b1, g), "c")
    g = add([((0, 2), s2), ((1, 1), t1)], g, b1, a2, y0)
    qa, q2 = passed(after(y0, g), "x"), swapped(after(a2, y0, g), "yl")
    c_y0 = swapped(after(y0, s3, g), "c")
    c_b1 = swapped(after(b1, c_a1, g), "c")
    t3 = passed(after(t2, g), "z")
    g = add([((0, 3), s3), ((1, 2), t2)], g, c_a1)
    qb = passed(after(c_y0, g), "x")
    c_a2 = swapped(after(a2, c_b1, g), "c")
    g = add([((1, 3), t3)], g, c_b1, c_y0)
    shape = (own.shape[0] * 4 * nx, density.shape[1])
    out, live = product(live, g, [
        ((0, 0, 0), (own,)), ((0, 0, 1), (c_own,)), ((0, 1, 0), (a1,)), ((0, 1, 1), (b1,)),
        ((1, 0, 0), (y0,)), ((1, 0, 1), (c_y0,)), ((0, -1, 1), (c_a1,)), ((0, -1, 0), (c_b1,)),
    ], out, shape, span, 0)
    c_qa = swapped(after(qa, live), "c")
    c_q2 = swapped(after(q2, live), "c")
    out, live = product(live, g, [
        ((0, 2, 0), (a2,)), ((0, 2, 1), (c_a2,)), ((1, 1, 0), (qa,)), ((1, 2, 0), (q2,)),
    ], out, shape, span)
    c_qb = swapped(after(qb, live), "c")
    out, live = product(live, g, [
        ((1, -1, 1), (c_qa,)), ((1, 2, 1), (c_q2,)), ((1, 1, 1), (qb,)),
    ], out, shape, span)
    out, live = product(live, g, [((1, -1, 0), (c_qb,))], out, shape, span)
    return out, live


def expand_keep(block_mask, row_live, col_live):
    wide = jnp.repeat(jnp.repeat(block_mask == 1, BLK, 0), BLK, 1)
    return wide & row_live[:, None] & col_live[None, :]


def ring(value, axes, count):
    return lax.ppermute(value, axes, [(i, (i + 1) % count) for i in range(count)])


def full_width(out, tensor, density, mask_t, density_mask, block_sizes):
    rows = lax.axis_size("yh") * lax.axis_size("z")
    cols = lax.axis_size("yl") * lax.axis_size("x") * lax.axis_size("c")
    row_at, col_at = at_row(), at_col()
    _, mu, nu = tensor.shape
    deep, sig = density.shape
    live = (jnp.arange(BLK)[None, :] < block_sizes[:, None]).reshape(-1)
    part = lax.dynamic_slice_in_dim
    own = jnp.where(
        expand_keep(part(mask_t, col_at * (mu // BLK), mu // BLK, 1).T, part(live, col_at * mu, mu), live[:nu]),
        tensor[0], jnp.zeros((), tensor.dtype),
    )
    mask = lax.dynamic_slice(
        density_mask, (row_at * (deep // BLK), col_at * (sig // BLK)), (deep // BLK, sig // BLK)
    )
    rho = jnp.where(
        expand_keep(mask, part(live, row_at * deep, deep), part(live, col_at * sig, sig)),
        density, jnp.zeros((), density.dtype),
    )

    def collect(i, carry):
        whole, panel = carry
        at = lax.rem(row_at - i + rows, rows) * deep
        return lax.dynamic_update_slice(whole, panel, (at, 0)), ring(panel, ROW, rows)

    whole, _ = lax.fori_loop(0, rows, collect, (jnp.zeros((nu, sig), rho.dtype), rho))

    def multiply(i, carry):
        total, chunk = carry
        at = lax.rem(col_at - i + cols, cols) * mu
        block = jnp.dot(chunk, whole, preferred_element_type=jnp.float32).astype(total.dtype)
        return lax.dynamic_update_slice(total, block, (at, 0)), ring(chunk, COL, cols)

    return lax.fori_loop(0, cols, multiply, (out, own))[0]


def local(*args):
    nu = args[0].shape[2]
    narrow = nu * 7 // 8
    out, live = contract(narrow, args[1].shape[1], None, *args)
    more = live[0, 0] > narrow
    mask_t = after(args[2], live).T

    def again(carry):
        return jnp.bool_(False), full_width(carry[1], *args[:2], mask_t, *args[3:])

    return lax.while_loop(lambda carry: carry[0], again, (more, out))[1][None]


def solution(mesh):
    rows, cols = mesh.devices.shape
    nz, nx, nc = rows // 2, cols // 4, 2
    fine = Mesh(mesh.devices.reshape(2, nz, 2, nx, nc), ("yh", "z", "yl", "x", "c"))
    placed = (P(ROW, COL, None), P(ROW, COL), P(), P(), P())
    return jax.shard_map(
        local, mesh=fine, in_specs=placed, out_specs=P(ROW, None, COL), check_vma=False
    )
```

```python
import functools

import jax
import jax.numpy as jnp
from jax import lax
from jax.experimental import pallas as pl
from jax.experimental.pallas import tpu as pltpu
from jax.sharding import Mesh, PartitionSpec as P

BLK = 128
ROW = ("yh", "z")
COL = ("yl", "x", "c")
MIB = 1024 * 1024
VMEM = pl.BlockSpec(memory_space=pltpu.VMEM)
SMEM = pl.BlockSpec(memory_space=pltpu.SMEM)
ANY = pl.BlockSpec(memory_space=pl.ANY)
HBM = pl.BlockSpec(memory_space=pltpu.HBM)
ROUND = pl.CostEstimate(flops=5 * 10**9, bytes_accessed=0, transcendentals=0)


def after(value, *earlier):
    return lax.optimization_barrier((value, *earlier))[0]


def passed(value, axis):
    n = lax.axis_size(axis)
    pairs = [(i * 2 + c, ((i + 1 - 2 * c) % n) * 2 + c) for i in range(n) for c in range(2)]
    return lax.ppermute(value, (axis, "c"), pairs)


def swapped(value, axis):
    return lax.ppermute(value, axis, [(0, 1), (1, 0)])


def offset_of(sizes_ref, count):
    return lax.fori_loop(0, count, lambda i, s: s + sizes_ref[i], jnp.int32(0))


def at_row():
    return lax.axis_index("yh") * lax.axis_size("z") + lax.axis_index("z")


def at_col():
    nx, nc = lax.axis_size("x"), lax.axis_size("c")
    return (lax.axis_index("yl") * nx + lax.axis_index("x")) * nc + lax.axis_index("c")


def wrapped(value, n):
    return lax.rem(value + n, n)


def chunk_place(dy, dx, dc):
    nx, c = lax.axis_size("x"), lax.axis_index("c")
    x = wrapped(lax.axis_index("x") - (1 - 2 * c) * dx, nx)
    return (wrapped(lax.axis_index("yl") + dy, 2) * nx + x) * 2 + wrapped(c + dc, 2)


def panel_place(dy, d):
    nz = lax.axis_size("z")
    z = wrapped(lax.axis_index("z") - (1 - 2 * lax.axis_index("c")) * d, nz)
    return wrapped(lax.axis_index("yh") + dy, 2) * nz + z


def start_body(sizes_hbm, t_mask_hbm, d_mask_hbm, tensor_hbm, density_hbm, own_ref, rho_ref,
               live_ref, sizes_ref, t_mask_ref, d_mask_ref, tensor_ref, density_ref, sem):
    copies = [
        pltpu.make_async_copy(src, dst, sem.at[i])
        for i, (src, dst) in enumerate([
            (sizes_hbm, sizes_ref), (t_mask_hbm, t_mask_ref), (d_mask_hbm, d_mask_ref),
            (density_hbm, density_ref), (tensor_hbm.at[0], tensor_ref),
        ])
    ]
    for copy in copies:
        copy.start()
    row_at, col_at = at_row(), at_col()
    wide = own_ref.shape[1]
    slot = lax.broadcasted_iota(jnp.int32, (BLK, 2 * BLK), 0)
    target = lax.broadcasted_iota(jnp.int32, (BLK, 2 * BLK), 1)
    row = lax.broadcasted_iota(jnp.int32, (BLK, BLK), 0)
    col = lax.broadcasted_iota(jnp.int32, (BLK, BLK), 1)
    own_ref[...] = jnp.zeros_like(own_ref)
    for copy in copies[:4]:
        copy.wait()
    rows, cols = rho_ref.shape
    for i in range(rows // BLK):
        nu = row_at * (rows // BLK) + i
        for j in range(cols // BLK):
            sig = col_at * (cols // BLK) + j
            live = jnp.where(d_mask_ref[nu, sig] == 1, sizes_ref[nu], 0)
            at = (pl.ds(i * BLK, BLK), pl.ds(j * BLK, BLK))
            part = density_ref[at].astype(jnp.float32)
            keep = (row < live) & (col < sizes_ref[sig])
            rho_ref[at] = jnp.where(keep, part, 0.0).astype(rho_ref.dtype)
    copies[4].wait()
    blocks = own_ref.shape[0] // BLK
    offset = jnp.int32(0)
    for n in range(tensor_ref.shape[1] // BLK):
        size = sizes_ref[n]
        start = jnp.minimum(offset // BLK * BLK, wide - 2 * BLK)
        start = pl.multiple_of(start, BLK)
        pick = (target == slot + (offset - start)) & (slot < size)
        pick = pick.astype(jnp.float32).astype(jnp.bfloat16)
        for m in range(blocks):
            mu = col_at * blocks + m
            live = jnp.where(t_mask_ref[n, mu] == 1, sizes_ref[mu], 0)
            at = pl.ds(m * BLK, BLK)
            part = tensor_ref[at, n * BLK : (n + 1) * BLK].astype(jnp.float32)
            part = jnp.where(row < live, part, 0.0).astype(jnp.bfloat16)
            moved = jnp.dot(part, pick, preferred_element_type=jnp.float32)
            own_ref[at, pl.ds(start, 2 * BLK)] += moved.astype(jnp.bfloat16)
        offset = offset + size
    live_ref[...] = jnp.full_like(live_ref, offset)


def start(sizes, t_mask, d_mask, tensor, density, wide):
    _, rows, nu = tensor.shape
    return pl.pallas_call(
        start_body,
        in_specs=[HBM] * 5,
        out_specs=[VMEM] * 3,
        out_shape=[
            jax.ShapeDtypeStruct((rows, wide), tensor.dtype),
            jax.ShapeDtypeStruct(density.shape, density.dtype),
            jax.ShapeDtypeStruct((8, BLK), jnp.int32),
        ],
        scratch_shapes=[
            pltpu.SMEM(sizes.shape, jnp.int32),
            pltpu.SMEM(t_mask.shape[::-1], jnp.int32),
            pltpu.SMEM(d_mask.shape, jnp.int32),
            pltpu.VMEM((rows, nu), tensor.dtype),
            pltpu.VMEM(density.shape, density.dtype),
            pltpu.SemaphoreType.DMA((5,)),
        ],
        compiler_params=pltpu.CompilerParams(vmem_limit_bytes=48 * MIB),
        cost_estimate=ROUND,
    )(sizes, t_mask.T, d_mask, tensor, density)


def in_spans(columns, total, span):
    if span == total:
        columns(0, 0)
    else:
        lax.fori_loop(0, total // span, columns, 0)


def gather_body(origins, first, span, sizes_hbm, *refs):
    panels = len(origins)
    out_ref, sizes_ref, sem = refs[panels + (0 if first else 1) :]
    copy = pltpu.make_async_copy(sizes_hbm, sizes_ref, sem)
    copy.start()
    rows = refs[0].shape[0]
    wide = out_ref.shape[0]
    window = rows + 16
    target = lax.broadcasted_iota(jnp.int32, (window, rows), 0)
    slot = lax.broadcasted_iota(jnp.int32, (window, rows), 1)
    if first:
        out_ref[...] = jnp.zeros_like(out_ref)
    per = rows // BLK
    copy.wait()
    for k, origin in enumerate(origins):
        at = panel_place(*origin) * per
        offset = offset_of(sizes_ref, at)
        start = pl.multiple_of(jnp.minimum(offset // 16 * 16, wide - window), 16)
        base = offset - start
        pick = jnp.zeros((window, rows), jnp.bool_)
        for b in range(per):
            size = sizes_ref[at + b]
            inside = (slot >= b * BLK) & (slot < b * BLK + size)
            pick = pick | (inside & (target == slot - b * BLK + base))
            base = base + size
        pick = pick.astype(jnp.float32).astype(jnp.bfloat16)

        def columns(n, carry):
            at = slice(None) if span == out_ref.shape[1] else pl.ds(pl.multiple_of(n * span, span), span)
            moved = jnp.dot(pick, refs[k][:, at], preferred_element_type=jnp.float32)
            out_ref[pl.ds(start, window), at] += moved.astype(out_ref.dtype)
            return carry

        in_spans(columns, out_ref.shape[1], span)


def gather(sizes, panels, wide, out, span):
    cols = panels[0][1].shape[1]
    first = out is None
    return pl.pallas_call(
        functools.partial(gather_body, [o for o, _ in panels], first, span),
        in_specs=[HBM] + [VMEM] * (len(panels) + (0 if first else 1)),
        out_specs=VMEM,
        out_shape=jax.ShapeDtypeStruct((wide, cols), jnp.bfloat16),
        scratch_shapes=[pltpu.SMEM(sizes.shape, jnp.int32), pltpu.SemaphoreType.DMA],
        input_output_aliases={} if first else {1 + len(panels): 0},
        compiler_params=pltpu.CompilerParams(vmem_limit_bytes=8 * MIB),
        cost_estimate=ROUND,
    )(sizes, *[p for _, p in panels], *([] if first else [out]))


def product_body(origins, first, span, live_ref, rho_ref, *refs):
    count = len(origins)
    a_refs = refs[:count]
    out_ref, token_ref, o_buf, o_sem = refs[count + (0 if first else 1) :]
    tall = o_buf.shape[1]

    def out_copy(i):
        start = pl.multiple_of(chunk_place(*origins[i]) * tall, tall)
        return pltpu.make_async_copy(
            o_buf.at[i % 2], out_ref.at[pl.ds(start, tall)], o_sem.at[i % 2]
        )

    for i in range(count):
        if i >= 2:
            out_copy(i - 2).wait()

        def columns(n, carry):
            at = slice(None) if span == out_ref.shape[1] else pl.ds(pl.multiple_of(n * span, span), span)
            o_buf[i % 2, :, at] = jnp.dot(
                a_refs[i][...], rho_ref[:, at], preferred_element_type=jnp.float32
            ).astype(o_buf.dtype)
            return carry

        in_spans(columns, o_buf.shape[2], span)
        out_copy(i).start()
    for i in range(max(count - 2, 0), count):
        out_copy(i).wait()
    token_ref[...] = live_ref[...]


def product(live, rho, chunks, out, shape, span, cost=1):
    flat = [part for _, (part,) in chunks]
    tall, wide = flat[0].shape
    count, first = len(chunks), out is None
    return pl.pallas_call(
        functools.partial(product_body, [o for o, _ in chunks], first, span),
        in_specs=[VMEM] * (2 + len(flat)) + ([] if first else [ANY]),
        out_specs=[ANY, VMEM],
        scratch_shapes=[
            pltpu.VMEM((2, tall, shape[1]), jnp.bfloat16),
            pltpu.SemaphoreType.DMA((2,)),
        ],
        out_shape=[
            jax.ShapeDtypeStruct(shape, jnp.bfloat16),
            jax.ShapeDtypeStruct(live.shape, live.dtype),
        ],
        input_output_aliases={} if first else {2 + len(flat): 0},
        compiler_params=pltpu.CompilerParams(vmem_limit_bytes=44 * MIB),
        cost_estimate=pl.CostEstimate(
            flops=2 * cost * count * tall * wide * shape[1],
            bytes_accessed=2 * cost * count * tall * shape[1],
            transcendentals=0,
        ),
    )(live, rho, *flat, *([] if first else [out]))


def early_body(count, rho_ref, *refs):
    sum_ref = refs[count]
    for i in range(count):
        sum_ref[i] = jnp.dot(refs[i][...], rho_ref[...], preferred_element_type=jnp.float32)


def early(rho, chunks):
    tall, wide = chunks[0].shape
    count, sig = len(chunks), rho.shape[1]
    return pl.pallas_call(
        functools.partial(early_body, count),
        in_specs=[VMEM] * (1 + count),
        out_specs=VMEM,
        out_shape=jax.ShapeDtypeStruct((count, tall, sig), jnp.float32),
        compiler_params=pltpu.CompilerParams(vmem_limit_bytes=8 * MIB),
        cost_estimate=pl.CostEstimate(
            flops=2 * count * tall * wide * sig, bytes_accessed=0, transcendentals=0
        ),
    )(rho, *chunks)


def finish_body(origins, panel_at, sizes_hbm, panel_ref, sum_ref, *refs):
    count = len(origins)
    out_ref, sizes_ref, late_ref, o_buf, sem, o_sem = refs[count:]
    copy = pltpu.make_async_copy(sizes_hbm, sizes_ref, sem)
    copy.start()
    rows, wide, tall = panel_ref.shape[0], refs[0].shape[1], o_buf.shape[1]
    per, window = rows // BLK, late_ref.shape[0]
    target = lax.broadcasted_iota(jnp.int32, (window, rows), 0)
    slot = lax.broadcasted_iota(jnp.int32, (window, rows), 1)
    copy.wait()
    at = panel_place(*panel_at) * per
    offset = offset_of(sizes_ref, at)
    start = pl.multiple_of(jnp.minimum(offset // BLK * BLK, wide - window), BLK)
    base = offset - start
    pick = jnp.zeros((window, rows), jnp.bool_)
    for b in range(per):
        size = sizes_ref[at + b]
        inside = (slot >= b * BLK) & (slot < b * BLK + size)
        pick = pick | (inside & (target == slot - b * BLK + base))
        base = base + size
    pick = pick.astype(jnp.float32).astype(jnp.bfloat16)
    moved = jnp.dot(pick, panel_ref[...], preferred_element_type=jnp.float32)
    late_ref[...] = moved.astype(late_ref.dtype)

    def out_copy(i):
        where = pl.multiple_of(chunk_place(*origins[i]) * tall, tall)
        return pltpu.make_async_copy(o_buf.at[i], out_ref.at[pl.ds(where, tall)], o_sem.at[i])

    for i in range(count):
        more = jnp.dot(
            refs[i][:, pl.ds(start, window)], late_ref[...], preferred_element_type=jnp.float32
        )
        o_buf[i] = (sum_ref[i] + more).astype(o_buf.dtype)
        out_copy(i).start()
    for i in range(count):
        out_copy(i).wait()


def finish(sizes, panel_at, panel, sums, chunks, shape):
    count, tall = len(chunks), sums.shape[1]
    return pl.pallas_call(
        functools.partial(finish_body, [o for o, _ in chunks], panel_at),
        in_specs=[HBM] + [VMEM] * (2 + count),
        out_specs=ANY,
        scratch_shapes=[
            pltpu.SMEM(sizes.shape, jnp.int32),
            pltpu.VMEM((panel.shape[0] + BLK, shape[1]), jnp.bfloat16),
            pltpu.VMEM((count, tall, shape[1]), jnp.bfloat16),
            pltpu.SemaphoreType.DMA,
            pltpu.SemaphoreType.DMA((count,)),
        ],
        out_shape=jax.ShapeDtypeStruct(shape, jnp.bfloat16),
        compiler_params=pltpu.CompilerParams(vmem_limit_bytes=38 * MIB),
        cost_estimate=pl.CostEstimate(flops=0, bytes_accessed=0, transcendentals=0),
    )(sizes, panel, sums, *[part for _, (part,) in chunks])


def contract(wide, span, out, tensor, density, tensor_mask, density_mask, block_sizes):
    nz, nx = lax.axis_size("z"), lax.axis_size("x")
    own, rho, live = start(block_sizes, tensor_mask, density_mask, tensor, density, wide)

    def add(panels, out, *earlier):
        return gather(after(block_sizes, *earlier), panels, wide, out, span)

    a1, c_own = passed(own, "x"), swapped(own, "c")
    s1, t0 = passed(rho, "z"), swapped(rho, "yh")
    y0 = swapped(own, "yl")
    g = add([((0, 0), rho)], None, own)
    b1 = passed(after(c_own, g), "x")
    s2 = passed(after(s1, g), "z")
    g = add([((0, 1), s1)], g, c_own)
    a2, t1 = passed(after(a1, g), "x"), passed(after(t0, g), "z")
    g = add([((1, 0), t0)], g, a1)
    s3, t2 = passed(after(s2, g), "z"), passed(after(t1, g), "z")
    c_a1 = swapped(after(a1, b1, g), "c")
    g = add([((0, 2), s2), ((1, 1), t1)], g, b1, a2, y0)
    qa, q2 = passed(after(y0, g), "x"), swapped(after(a2, y0, g), "yl")
    c_y0 = swapped(after(y0, s3, g), "c")
    c_b1 = swapped(after(b1, c_a1, g), "c")
    t3 = passed(after(t2, g), "z")
    g = add([((0, 3), s3), ((1, 2), t2)], g, c_a1)
    qb = passed(after(c_y0, g), "x")
    c_a2 = swapped(after(a2, c_b1, g), "c")
    sums = early(after(g, c_b1, c_y0), [own, c_own, a1, b1])
    g = add([((1, 3), t3)], g)
    shape = (own.shape[0] * 4 * nx, density.shape[1])
    ready = [((0, 0, 0), (own,)), ((0, 0, 1), (c_own,)), ((0, 1, 0), (a1,)), ((0, 1, 1), (b1,))]
    out = finish(block_sizes, (1, 3), t3, sums, ready, shape)
    out, live = product(live, g, [
        ((1, 0, 0), (y0,)), ((1, 0, 1), (c_y0,)), ((0, -1, 1), (c_a1,)), ((0, -1, 0), (c_b1,)),
    ], out, shape, span, 0)
    c_qa = swapped(after(qa, live), "c")
    c_q2 = swapped(after(q2, live), "c")
    out, live = product(live, g, [
        ((0, 2, 0), (a2,)), ((0, 2, 1), (c_a2,)), ((1, 1, 0), (qa,)), ((1, 2, 0), (q2,)),
    ], out, shape, span)
    c_qb = swapped(after(qb, live), "c")
    out, live = product(live, g, [
        ((1, -1, 1), (c_qa,)), ((1, 2, 1), (c_q2,)), ((1, 1, 1), (qb,)),
    ], out, shape, span)
    out, live = product(live, g, [((1, -1, 0), (c_qb,))], out, shape, span)
    return out, live


def expand_keep(block_mask, row_live, col_live):
    wide = jnp.repeat(jnp.repeat(block_mask == 1, BLK, 0), BLK, 1)
    return wide & row_live[:, None] & col_live[None, :]


def ring(value, axes, count):
    return lax.ppermute(value, axes, [(i, (i + 1) % count) for i in range(count)])


def full_width(out, tensor, density, mask_t, density_mask, block_sizes):
    rows = lax.axis_size("yh") * lax.axis_size("z")
    cols = lax.axis_size("yl") * lax.axis_size("x") * lax.axis_size("c")
    row_at, col_at = at_row(), at_col()
    _, mu, nu = tensor.shape
    deep, sig = density.shape
    live = (jnp.arange(BLK)[None, :] < block_sizes[:, None]).reshape(-1)
    part = lax.dynamic_slice_in_dim
    own = jnp.where(
        expand_keep(part(mask_t, col_at * (mu // BLK), mu // BLK, 1).T, part(live, col_at * mu, mu), live[:nu]),
        tensor[0], jnp.zeros((), tensor.dtype),
    )
    mask = lax.dynamic_slice(
        density_mask, (row_at * (deep // BLK), col_at * (sig // BLK)), (deep // BLK, sig // BLK)
    )
    rho = jnp.where(
        expand_keep(mask, part(live, row_at * deep, deep), part(live, col_at * sig, sig)),
        density, jnp.zeros((), density.dtype),
    )

    def collect(i, carry):
        whole, panel = carry
        at = lax.rem(row_at - i + rows, rows) * deep
        return lax.dynamic_update_slice(whole, panel, (at, 0)), ring(panel, ROW, rows)

    whole, _ = lax.fori_loop(0, rows, collect, (jnp.zeros((nu, sig), rho.dtype), rho))

    def multiply(i, carry):
        total, chunk = carry
        at = lax.rem(col_at - i + cols, cols) * mu
        block = jnp.dot(chunk, whole, preferred_element_type=jnp.float32).astype(total.dtype)
        return lax.dynamic_update_slice(total, block, (at, 0)), ring(chunk, COL, cols)

    return lax.fori_loop(0, cols, multiply, (out, own))[0]


def local(*args):
    nu = args[0].shape[2]
    narrow = nu * 7 // 8
    out, live = contract(narrow, args[1].shape[1], None, *args)
    more = live[0, 0] > narrow
    mask_t = after(args[2], live).T

    def again(carry):
        return jnp.bool_(False), full_width(carry[1], *args[:2], mask_t, *args[3:])

    return lax.while_loop(lambda carry: carry[0], again, (more, out))[1][None]


def solution(mesh):
    rows, cols = mesh.devices.shape
    nz, nx, nc = rows // 2, cols // 4, 2
    fine = Mesh(mesh.devices.reshape(2, nz, 2, nx, nc), ("yh", "z", "yl", "x", "c"))
    placed = (P(ROW, COL, None), P(ROW, COL), P(), P(), P())
    return jax.shard_map(
        local, mesh=fine, in_specs=placed, out_specs=P(ROW, None, COL), check_vma=False
    )
```
